128 devices in a mesh: pass: 64 (over x_hi, z, y, core), qry: 2 (over x_lo).
Axes of the slice: x: 4 (x_hi: 2, x_lo: 2; x = x_hi * 2 + x_lo), y: 4, z: 4, core: 2. Of those that a mesh axis runs over, the one named last changes fastest.
Arguments:
- student_queries: bfloat16 [4096, 768], P('qry'), may hold values from -8 to 8
- teacher_queries: bfloat16 [4096, 1024], P('qry'), may hold values from -8 to 8
- student_passages: bfloat16 [65536, 768], P('pass'), may hold values from -8 to 8
- teacher_passages: bfloat16 [65536, 1024], P('pass'), may hold values from -8 to 8
- positives: int32 [4096], P('qry'), may hold values from 0 to 65535
Outputs:
- loss: float32 [], replicated
- grad_queries: float32 [4096, 768], P('qry')
- grad_passages: float32 [65536, 768], P(('pass', 'qry'))
The draws below stay inside these ranges and needn't reach their ends.
All inputs are finite; a program needn't handle non-finite values.
Results may differ from the reference program's by a relative error of at most 0.0026.
Values sent between devices are 32-bit elements; how exact they have to be, the bound alone decides.
A program may use at most 128 MiB of HBM per device.

```python
import math
import jax
import jax.numpy as jnp
import numpy as np
from jax import lax

DS = 768
DT = 1024
QUERIES = 4096
PASSAGES = 65536


peak_targets = (230.0, 260.0, 290.0, 320.0)


def peak_vectors(key, width):
    signs = jax.random.rademacher(jax.random.fold_in(key, 900 + width), (4, width), jnp.float32)
    targets = jnp.array(peak_targets, jnp.float32)[:, None]
    magnitude = jnp.sqrt(targets / (3.0 * math.sqrt(width)))
    return signs * magnitude


def drawn_rows(key, rows, width):
    return jnp.clip(jax.random.normal(key, (rows, width), jnp.float32), -4.0, 4.0)


def rising_rows(key, values, rows, low_end, high_end):
    position = jnp.arange(rows, dtype=jnp.float32) / max(rows - 1, 1)
    trend = jnp.exp(math.log(low_end) + position * (math.log(high_end) - math.log(low_end)))
    jitter = jnp.exp(jax.random.uniform(jax.random.fold_in(key, 77), (rows,), jnp.float32, math.log(0.8), math.log(1.25)))
    return jnp.clip(values * (trend * jitter)[:, None], -8.0, 8.0)


def place_query_peaks(shared, values, width):
    places = np.arange(4) * (QUERIES // 4)
    return values.at[places].set(peak_vectors(shared, width))


def place_passage_peaks(shared, values, width):
    places = np.arange(4) * (PASSAGES // 4) + 1
    peaks = peak_vectors(shared, width)
    shrink = 1.0 - 2.0 / jnp.array(peak_targets, jnp.float32)[:, None]
    values = values.at[places].set(peaks)
    return values.at[places + 1].set(peaks * shrink)


def draw_student_queries(key, part):
    shared = key
    key = jax.random.fold_in(key, 1)
    values = drawn_rows(key, QUERIES, DS)
    values = rising_rows(key, values, QUERIES, 0.4, 2.0)
    return place_query_peaks(shared, values, DS).astype(jnp.bfloat16)


def draw_teacher_queries(key, part):
    shared = key
    key = jax.random.fold_in(key, 2)
    values = drawn_rows(key, QUERIES, DT)
    return place_query_peaks(shared, values, DT).astype(jnp.bfloat16)


def draw_student_passages(key, part):
    shared = key
    key = jax.random.fold_in(key, 3)
    values = drawn_rows(key, PASSAGES, DS)
    return place_passage_peaks(shared, values, DS).astype(jnp.bfloat16)


def draw_teacher_passages(key, part):
    shared = key
    key = jax.random.fold_in(key, 4)
    values = drawn_rows(key, PASSAGES, DT)
    return place_passage_peaks(shared, values, DT).astype(jnp.bfloat16)


def plant(values, own_key, low, high):
    place = [jax.random.randint(jax.random.fold_in(own_key, axis), (), 0, length) for axis, length in enumerate(values.shape)]
    main_axis = values.shape.index(max(values.shape))
    next_to = place[:main_axis] + [(place[main_axis] + 1) % values.shape[main_axis]] + place[main_axis + 1:]
    return values.at[tuple(place)].set(low).at[tuple(next_to)].set(high)


def setup_inputs(seed: int = 0) -> dict:
    arg_keys = jax.random.split(jax.random.key(seed), 6)
    student_queries = draw_student_queries(jax.random.fold_in(arg_keys[5], 71), 0)
    teacher_queries = draw_teacher_queries(jax.random.fold_in(arg_keys[5], 71), 0)
    student_passages = draw_student_passages(jax.random.fold_in(arg_keys[5], 71), 0)
    teacher_passages = draw_teacher_passages(jax.random.fold_in(arg_keys[5], 71), 0)
    positives = plant(jax.random.randint(arg_keys[4], (QUERIES,), 0, PASSAGES), jax.random.fold_in(arg_keys[4], 1), 0, PASSAGES - 1).astype(jnp.int32)
    return dict(student_queries=student_queries, teacher_queries=teacher_queries, student_passages=student_passages, teacher_passages=teacher_passages, positives=positives)


LOGIT_GAIN = 3.0
CE_WEIGHT = 0.5

def block_terms(query_block, teacher_block, positive_block, student_passages, teacher_passages):
    student_scale = LOGIT_GAIN / math.sqrt(query_block.shape[1])
    teacher_scale = LOGIT_GAIN / math.sqrt(teacher_block.shape[1])
    student_logits = jnp.dot(query_block, student_passages.T, preferred_element_type=jnp.float32) * student_scale
    teacher_logits = jnp.dot(teacher_block, teacher_passages.T, preferred_element_type=jnp.float32) * teacher_scale
    student_peak = lax.optimization_barrier(jnp.max(student_logits, axis=1))
    teacher_peak = lax.optimization_barrier(jnp.max(teacher_logits, axis=1))
    student_lse = student_peak + jnp.log(lax.optimization_barrier(jnp.sum(jnp.exp(student_logits - student_peak[:, None]), axis=1)))
    teacher_lse = teacher_peak + jnp.log(lax.optimization_barrier(jnp.sum(jnp.exp(teacher_logits - teacher_peak[:, None]), axis=1)))
    student_probs = jnp.exp(student_logits - student_lse[:, None])
    teacher_probs = jnp.exp(teacher_logits - teacher_lse[:, None])
    cross = lax.optimization_barrier(jnp.sum(teacher_probs * (teacher_logits - student_logits), axis=1))
    columns = jnp.arange(student_logits.shape[1], dtype=jnp.int32)
    is_positive = columns[None, :] == positive_block[:, None]
    positive_logit = lax.optimization_barrier(jnp.sum(jnp.where(is_positive, student_logits, 0.0), axis=1))
    row_loss = cross - teacher_lse + student_lse + CE_WEIGHT * (student_lse - positive_logit)
    logit_grads = ((1.0 + CE_WEIGHT) * student_probs - teacher_probs - CE_WEIGHT * is_positive.astype(jnp.float32)).astype(jnp.bfloat16)
    query_grads = jnp.dot(logit_grads, student_passages, preferred_element_type=jnp.float32) * student_scale
    passage_terms = lax.dot_general(logit_grads, query_block, (((0,), (0,)), ((), ())), preferred_element_type=jnp.float32) * student_scale
    return (row_loss, query_grads, passage_terms)

def reference(student_queries, teacher_queries, student_passages, teacher_passages, positives):
    block_rows = math.gcd(QUERIES, 128)
    blocks = QUERIES // block_rows
    query_blocks = student_queries.reshape(blocks, block_rows, DS)
    teacher_blocks = teacher_queries.reshape(blocks, block_rows, DT)
    positive_blocks = positives.reshape(blocks, block_rows)

    def advance(total, pieces):
        row_loss, query_grads, passage_terms = block_terms(pieces[0], pieces[1], pieces[2], student_passages, teacher_passages)
        return (total + passage_terms, (row_loss, query_grads))
    start_total = jnp.zeros((PASSAGES, DS), jnp.float32)
    passage_sum, (losses, query_grads) = lax.scan(advance, start_total, (query_blocks, teacher_blocks, positive_blocks))
    loss = jnp.sum(losses) / QUERIES
    return (loss, query_grads.reshape(QUERIES, DS), passage_sum * PASSAGES)
```

```python
import functools
import math

import jax
import jax.numpy as jnp
from jax import lax
from jax.experimental import pallas as pl
from jax.experimental.pallas import tpu as pltpu
from jax.sharding import PartitionSpec as P

LOGIT_GAIN = 3.0
CE_WEIGHT = 0.5
LOG2E = math.log2(math.e)
LN2 = math.log(2.0)
MESH = pl.DeviceIdType.MESH
NT = (((1,), (1,)), ((), ()))
TN = (((0,), (0,)), ((), ()))
NN = (((1,), (0,)), ((), ()))
TILE = 256
CHUNK = 512
CHUNKS = 4
STATS = 8


def dot(a, b, dims):
    return lax.dot_general(a, b, dims, preferred_element_type=jnp.float32)


def aligned(x, m):
    return x if isinstance(x, int) else pl.multiple_of(x, m)


def wide(rows):
    return jnp.concatenate([rows[k : k + 1, :] for k in range(rows.shape[0])], axis=1)


def log_total(values):
    peak = functools.reduce(jnp.maximum, values)
    total = functools.reduce(jnp.add, [jnp.exp2(v - peak) for v in values])
    return peak + jnp.log(total) * LOG2E


def kernel(
    sq_hbm, tq_hbm, sp_hbm, tp_hbm, pos_ref, loss_ref, out, pas,
    sq, tq, sp, tp, es, et, stat, bs0, bt0, mx0, bs1, bt1, mx1, g, own, half, rfar, rnear, rx, ps, pr,
    sb1, s1, sb2, s2, lse, lb1, lb2, lb3, lacc, ssem, rsem, lsem,
):
    queries, ds = sq.shape
    passages, dt = tp.shape
    cs = LOGIT_GAIN / math.sqrt(ds) * LOG2E
    ct = LOGIT_GAIN / math.sqrt(dt) * LOG2E
    scale = LOGIT_GAIN / math.sqrt(ds)
    tiles = passages // TILE
    p, q = lax.axis_index("pass"), lax.axis_index("qry")
    core, y, z, xh = p % 2, (p // 2) % 4, (p // 8) % 4, p // 32

    def dev(c=core, yy=y, zz=z, x=xh, qq=q):
        return (((x * 4 + zz) * 4 + yy) * 2 + c, qq)

    loads = {}

    def load(name, src, dst):
        loads[name] = pltpu.make_async_copy(src, dst, lsem.at[len(loads)])
        loads[name].start()

    def rows(c):
        return pl.ds(c * CHUNK, CHUNK)

    load("sp", sp_hbm, sp)
    load("sq0", sq_hbm.at[rows(0)], sq.at[rows(0)])
    load("tp", tp_hbm, tp)
    load("tq0", tq_hbm.at[rows(0)], tq.at[rows(0)])
    for c in range(1, CHUNKS):
        load(f"sq{c}", sq_hbm.at[rows(c)], sq.at[rows(c)])
        load(f"tq{c}", tq_hbm.at[rows(c)], tq.at[rows(c)])

    group1 = [(a, b) for a in range(2) for b in range(4) if (a, b) != (0, 0)]
    peers1 = [dev(c=(core + a) % 2, yy=(y + b) % 4) for a, b in group1]
    peers2 = [dev(x=(xh + a) % 2, zz=(z + b) % 4) for a, b in group1]
    partner = dev(c=1 - core)
    across = dev(x=1 - xh)
    other = dev(qq=1 - q)
    barrier = pltpu.get_barrier_semaphore()
    everyone = peers1 + peers2 + [other]
    for peer in everyone:
        pl.semaphore_signal(barrier, inc=1, device_id=peer, device_id_type=MESH)

    counts = {"sem": 0}
    sent = []

    def sem():
        counts["sem"] += 1
        return counts["sem"] - 1

    def send(src, dst, peer, i=None):
        i = sem() if i is None else i
        copy = pltpu.make_async_remote_copy(
            src_ref=src, dst_ref=dst, send_sem=ssem.at[i], recv_sem=rsem.at[i], device_id=peer, device_id_type=MESH
        )
        copy.start()
        return copy

    def post(src, dst, peer):
        copy = send(src, dst, peer)
        sent.append(copy)
        return copy

    def spread(src, slots, peers, each):
        i = sem()
        for n, peer in enumerate(peers):
            send(src, each(n), peer, i)
        whole = slots.at[pl.ds(0, STATS - 1)]
        both = pltpu.make_async_remote_copy(
            src_ref=whole, dst_ref=whole, send_sem=ssem.at[i], recv_sem=rsem.at[i], device_id=peers[0], device_id_type=MESH
        )
        sent.append(both)
        return both

    buffers = ((bs0, bt0, mx0), (bs1, bt1, mx1))

    def products(i, piece):
        c, t = divmod(i, tiles)
        bs, bt, mx = buffers[i % 2]
        teacher, j = divmod(piece, 2)
        w = CHUNK // 2
        if t == 0 and j == 0:
            if c == 0:
                loads["tp" if teacher else "sp"].wait()
            loads[f"{'tq' if teacher else 'sq'}{c}"].wait()
        a = (tp if teacher else sp)[pl.ds(t * TILE, TILE), :]
        b = (tq if teacher else sq)[pl.ds(c * CHUNK + j * w, w), :]
        r = dot(a, b, NT)
        (bt if teacher else bs)[:, j * w : (j + 1) * w] = r
        mx[teacher, :, j * w : (j + 1) * w] = jnp.max(r.reshape(TILE // 8, 8, w), axis=0)

    def exponentials(i, j):
        c, t = divmod(i, tiles)
        bs, bt, mx = buffers[i % 2]
        w = CHUNK // 2
        cut = slice(j * w, (j + 1) * w)
        d = pl.ds(c * CHUNK + j * w, w)
        s2 = bs[:, cut] * cs
        t2 = bt[:, cut] * ct
        ms = jnp.max(mx[0, :, cut], axis=0, keepdims=True) * cs
        mt = jnp.max(mx[1, :, cut], axis=0, keepdims=True) * ct
        e_s = jnp.exp2(s2 - ms)
        e_t = jnp.exp2(t2 - mt)
        row = lax.broadcasted_iota(jnp.int32, (TILE, w), 0) + t * TILE
        at_positive = jnp.where(row == pos_ref[0:1, d] - p * passages, s2, 0.0)
        es[pl.ds(t * TILE, TILE), d] = e_s
        et[pl.ds(t * TILE, TILE), d] = e_t
        stat[t, 0:1, d] = ms
        stat[t, 1:2, d] = mt
        stat[t, 2:3, d] = jnp.sum(e_s, axis=0, keepdims=True)
        stat[t, 3:4, d] = jnp.sum(e_t, axis=0, keepdims=True)
        stat[t, 4:5, d] = jnp.sum(e_t * (t2 - s2), axis=0, keepdims=True)
        stat[t, 5:6, d] = jnp.sum(at_positive, axis=0, keepdims=True)

    def logits(c):
        for i in range(c * tiles, (c + 1) * tiles):
            for j in range(4):
                if i + 1 < CHUNKS * tiles:
                    products(i + 1, j)
                if j % 2 == 0:
                    exponentials(i, j // 2)

    waits1, waits2 = {}, {}

    def stats_local(c):
        d = rows(c)
        for k in range(2):
            peaks = [stat[t, k : k + 1, d] for t in range(tiles)]
            sums = [stat[t, 2 + k : 3 + k, d] for t in range(tiles)]
            peak = functools.reduce(jnp.maximum, peaks)
            total = functools.reduce(jnp.add, [s * jnp.exp2(m - peak) for s, m in zip(sums, peaks)])
            value = peak + jnp.log(total) * LOG2E
            for n in range(4):
                sb1[c, 4 * k + n : 4 * k + n + 1, :] = value[:, n * 128 : (n + 1) * 128]
        waits1[c] = spread(sb1.at[c], s1.at[c], peers1, lambda n: s1.at[c, n])

    def stats_middle(c):
        waits1[c].wait_recv()
        sb2[c] = log_total([sb1[c]] + [s1[c, n] for n in range(STATS - 1)])
        waits2[c] = spread(sb2.at[c], s2.at[c], peers2, lambda n: s2.at[c, n])

    def stats_final(c):
        waits2[c].wait_recv()
        lse[c] = log_total([sb2[c]] + [s2[c, n] for n in range(STATS - 1)])
        d = rows(c)
        lse_s, lse_t = wide(lse[c, 0:4, :]), wide(lse[c, 4:8, :])
        part = (1.5 * lse_s - lse_t) * (1.0 / 64.0)
        for t in range(tiles):
            part = part + stat[t, 4:5, d] * jnp.exp2(stat[t, 1:2, d] - lse_t) - CE_WEIGHT * stat[t, 5:6, d]
            stat[t, 6:7, d] = (1.0 + CE_WEIGHT) * jnp.exp2(stat[t, 0:1, d] - lse_s)
            stat[t, 7:8, d] = jnp.exp2(stat[t, 1:2, d] - lse_t)
        lacc[c : c + 1, :] = part

    def logit_grads(c):
        d = rows(c)
        positive = pos_ref[0:1, d] - p * passages

        @pl.loop(0, tiles)
        def _(t):
            r = pl.ds(pl.multiple_of(t * TILE, TILE), TILE)
            row = lax.broadcasted_iota(jnp.int32, (TILE, CHUNK), 0) + t * TILE
            v = es[r, d] * stat[t, 6:7, d] - et[r, d] * stat[t, 7:8, d]
            g[r, d] = jnp.where(row == positive, v - CE_WEIGHT, v).astype(jnp.bfloat16)

    def query_terms(c):
        own[rows(c), :] = dot(g[:, rows(c)], sp[...], TN)

    pas_rows = passages // 2
    pas_sent = []

    def passage_send(b):
        n = TILE
        ps[pl.ds(b * n, n), :] = dot(g[pl.ds(pl.multiple_of((1 - q) * pas_rows + b * n, n), n), :], sq[...], NN)
        pas_sent.append(post(ps.at[pl.ds(b * n, n)], pr.at[pl.ds(b * n, n)], other))

    def passage_own(b):
        n = TILE
        pas[pl.ds(b * n, n), :] = dot(g[pl.ds(pl.multiple_of(q * pas_rows + b * n, n), n), :], sq[...], NN)

    def passage_add(b):
        n = TILE
        pas_sent[b].wait_recv()
        r = pl.ds(b * n, n)
        pas[r, :] = (pas[r, :] + pr[r, :]) * (scale * passages * lax.axis_size("pass"))

    size = queries // CHUNKS
    piece, block, slab = size // 16, size // 64, size // 4
    hp = piece // 2

    def query_sum(c):
        base = c * size // 2

        def cut(s, j, h=None):
            at = base + s * slab + j * piece + (0 if h is None else h * hp)
            return half.at[pl.ds(aligned(at, hp), piece if h is None else hp)]

        def add(ref, *others):
            ref[...] = functools.reduce(jnp.add, [o[...] for o in others], ref[...])

        def far(s, k):
            return rfar.at[pl.ds(((c * 2 + s) * 6 + k) * hp, hp)]

        index = ((y, z), (z, y))

        def step(s, axis, d):
            along_y = (s == 0) == (axis == 0)
            return dev(yy=(y + d) % 4) if along_y else dev(zz=(z + d) % 4)

        first = post(
            own.at[pl.ds(aligned(c * size + (1 - core) * (size // 2), size // 2), size // 2)],
            half.at[pl.ds(base, size // 2)],
            partner,
        )
        yield
        first.wait_recv()
        mine = pl.ds(aligned(c * size + core * (size // 2), size // 2), size // 2)
        half[pl.ds(base, size // 2), :] = half[pl.ds(base, size // 2), :] + own[mine, :]
        w = {}
        for s in range(2):
            i = index[s][0]
            right, left = step(s, 0, 1), step(s, 0, 3)
            w[s, 0] = post(cut(s, (i + 2) % 4, 0), far(s, 0), right)
            w[s, 1] = post(cut(s, (i + 2) % 4, 1), far(s, 1), left)
            w[s, 2] = post(cut(s, (i + 1) % 4, 1), far(s, 2), right)
            w[s, 3] = post(cut(s, (i + 3) % 4, 0), far(s, 3), left)
        yield
        for s in range(2):
            i = index[s][0]
            right, left = step(s, 0, 1), step(s, 0, 3)
            w[s, 0].wait_recv()
            add(cut(s, (i + 1) % 4, 0), far(s, 0))
            w[s, 4] = post(cut(s, (i + 1) % 4, 0), far(s, 4), right)
            w[s, 1].wait_recv()
            add(cut(s, (i + 3) % 4, 1), far(s, 1))
            w[s, 5] = post(cut(s, (i + 3) % 4, 1), far(s, 5), left)
        yield

        def near(s, d):
            return rnear.at[pl.ds(((c * 2 + s) * 3 + d - 1) * block, block)]

        def small(s, j):
            at = base + s * slab + index[s][0] * piece + j * block
            return half.at[pl.ds(aligned(at, block), block)]

        for s in range(2):
            i, j = index[s]
            for k in range(2, 6):
                w[s, k].wait_recv()
            add(cut(s, i, 0), far(s, 3), far(s, 4))
            add(cut(s, i, 1), far(s, 2), far(s, 5))
            for d in range(1, 4):
                w[s, 5 + d] = post(small(s, (j + d) % 4), near(s, d), step(s, 1, d))
        yield

        def over(s):
            return rx.at[pl.ds((c * 2 + s) * block, block)]

        for s in range(2):
            j = index[s][1]
            for d in range(1, 4):
                w[s, 5 + d].wait_recv()
            add(small(s, j), *[near(s, d) for d in range(1, 4)])
            w[s, 9] = post(small(s, j), over(s), across)
        yield

        def place(s, i, j=0, n=piece):
            at = c * size + core * (size // 2) + s * slab + i * piece + j * block
            return out.at[pl.ds(aligned(at, min(n, block)), n)]

        for s in range(2):
            i, j = index[s]
            w[s, 9].wait_recv()
            here = place(s, i, j, block)
            here[...] = (small(s, j)[...] + over(s)[...]) * scale
            for d in range(1, 4):
                w[s, 9 + d] = post(here, here, step(s, 1, d))
        yield
        for s in range(2):
            i = index[s][0]
            for d in range(1, 4):
                w[s, 9 + d].wait_recv()
            w[s, 13] = post(place(s, i), place(s, i), step(s, 0, 1))
            w[s, 14] = post(place(s, i), place(s, i), step(s, 0, 3))
        yield

        def part(s, i, h):
            at = c * size + core * (size // 2) + s * slab + i * piece + h * hp
            return out.at[pl.ds(aligned(at, hp), hp)]

        for s in range(2):
            i = index[s][0]
            w[s, 13].wait_recv()
            w[s, 15] = post(part(s, (i + 3) % 4, 0), part(s, (i + 3) % 4, 0), step(s, 0, 1))
            w[s, 14].wait_recv()
            w[s, 16] = post(part(s, (i + 1) % 4, 1), part(s, (i + 1) % 4, 1), step(s, 0, 3))
        yield
        for s in range(2):
            w[s, 15].wait_recv()
            w[s, 16].wait_recv()
            done = out.at[pl.ds(aligned(c * size + core * (size // 2) + s * slab, slab), slab)]
            w[s, 17] = post(done, done, partner)
        yield
        for s in range(2):
            w[s, 17].wait_recv()
        yield

    def loss_sum():
        i1, i2 = core * 4 + y, xh * 4 + z
        total = jnp.sum(lacc[0:CHUNKS, :], axis=0, keepdims=True)
        total = functools.reduce(jnp.add, [total[:, n * 128 : (n + 1) * 128] for n in range(CHUNK // 128)])
        lb1[i1] = jnp.broadcast_to(total, (8, 128))
        wait = spread(lb1.at[i1], lb1, peers1, lambda n: lb1.at[i1])
        yield
        wait.wait_recv()
        lb2[i2] = functools.reduce(jnp.add, [lb1[n] for n in range(STATS)])
        wait = spread(lb2.at[i2], lb2, peers2, lambda n: lb2.at[i2])
        yield
        wait.wait_recv()
        lb3[0] = functools.reduce(jnp.add, [lb2[n] for n in range(STATS)])
        last = post(lb3.at[0], lb3.at[1], other)
        yield
        last.wait_recv()
        value = jnp.sum(lb3[0, 0:1, :] + lb3[1, 0:1, :], axis=1, keepdims=True) * (LN2 / (2 * queries))
        loss_ref[...] = jnp.broadcast_to(value, loss_ref.shape)
        yield

    for j in range(4):
        products(0, j)
    for c in range(CHUNKS):
        logits(c)
        if c == 0:
            pl.semaphore_wait(barrier, len(everyone))
        stats_local(c)
        if c >= 1:
            stats_middle(c - 1)
    sums = [query_sum(c) for c in range(CHUNKS)]
    loss = loss_sum()

    def compute(c):
        stats_final(c)
        logit_grads(c)
        query_terms(c)
        next(sums[c])

    compute(0)
    stats_middle(CHUNKS - 1)
    compute(1)
    next(sums[0])
    compute(2)
    next(sums[1])
    compute(3)
    next(sums[2])
    next(sums[0])
    for b in range(2):
        passage_send(b)
        next(sums[3 - 2 * b])
    next(loss)
    for b in range(2):
        passage_own(b)
        next(sums[b])
    stages = {0: 4, 1: 4, 2: 2, 3: 2}
    for tick in range(4, 20):
        for c in range(CHUNKS):
            while stages[c] < 10 and stages[c] + 2 * c <= tick:
                next(sums[c])
                stages[c] += 1
        if 6 <= tick < 9:
            next(loss)
    passage_add(0)
    passage_add(1)
    for copy in sent:
        copy.wait_send()


def shards(student_queries, teacher_queries, student_passages, teacher_passages, positives):
    queries, ds = student_queries.shape
    passages, dt = teacher_passages.shape
    f32, bf16 = jnp.float32, jnp.bfloat16
    vmem = pltpu.VMEM
    size = queries // CHUNKS
    scratch = [
        vmem((queries, ds), bf16),
        vmem((queries, dt), bf16),
        vmem((passages, ds), bf16),
        vmem((passages, dt), bf16),
        vmem((passages, queries), f32),
        vmem((passages, queries), f32),
        vmem((passages // TILE, 8, queries), f32),
        *[vmem((TILE, CHUNK), f32), vmem((TILE, CHUNK), f32), vmem((2, 8, CHUNK), f32)] * 2,
        vmem((passages, queries), bf16),
        vmem((queries, ds), f32),
        vmem((queries // 2, ds), f32),
        vmem((CHUNKS * 2 * 6 * (size // 32), ds), f32),
        vmem((CHUNKS * 2 * 3 * (size // 64), ds), f32),
        vmem((CHUNKS * 2 * (size // 64), ds), f32),
        vmem((passages // 2, ds), f32),
        vmem((passages // 2, ds), f32),
        vmem((CHUNKS, 8, 128), f32),
        vmem((CHUNKS, STATS - 1, 8, 128), f32),
        vmem((CHUNKS, 8, 128), f32),
        vmem((CHUNKS, STATS - 1, 8, 128), f32),
        vmem((CHUNKS, 8, 128), f32),
        vmem((STATS, 8, 128), f32),
        vmem((STATS, 8, 128), f32),
        vmem((2, 8, 128), f32),
        vmem((8, CHUNK), f32),
        pltpu.SemaphoreType.DMA((180,)),
        pltpu.SemaphoreType.DMA((180,)),
        pltpu.SemaphoreType.DMA((2 + 2 * CHUNKS,)),
    ]
    loss, query_grads, passage_grads = pl.pallas_call(
        kernel,
        out_shape=(
            jax.ShapeDtypeStruct((8, 128), f32),
            jax.ShapeDtypeStruct((queries, ds), f32),
            jax.ShapeDtypeStruct((passages // 2, ds), f32),
        ),
        in_specs=[pl.BlockSpec(memory_space=pl.ANY)] * 4 + [pl.BlockSpec(memory_space=vmem)],
        out_specs=[pl.BlockSpec(memory_space=vmem)] * 3,
        scratch_shapes=scratch,
        compiler_params=pltpu.CompilerParams(collective_id=0, has_side_effects=True, vmem_limit_bytes=62 * 2**20),
        cost_estimate=pl.CostEstimate(flops=14 * 10**9, bytes_accessed=20 * 10**6, transcendentals=4 * 10**6),
    )(student_queries, teacher_queries, student_passages, teacher_passages, positives.reshape(1, queries))
    return loss[0, 0], query_grads, passage_grads


def solution(mesh):
    return jax.shard_map(
        shards,
        mesh=mesh,
        in_specs=(P("qry", None), P("qry", None), P("pass", None), P("pass", None), P("qry")),
        out_specs=(P(), P("qry", None), P(("pass", "qry"), None)),
        check_vma=False,
    )
```

```python
import functools
import math

import jax
import jax.numpy as jnp
from jax import lax
from jax.experimental import pallas as pl
from jax.experimental.pallas import tpu as pltpu
from jax.sharding import PartitionSpec as P

LOGIT_GAIN = 3.0
CE_WEIGHT = 0.5
LOG2E = math.log2(math.e)
LN2 = math.log(2.0)
MESH = pl.DeviceIdType.MESH
NT = (((1,), (1,)), ((), ()))
TN = (((0,), (0,)), ((), ()))
NN = (((1,), (0,)), ((), ()))
TILE = 256
CHUNK = 512
CHUNKS = 4
STATS = 8
ROUNDS = 2
PARTS = (128, 64, 128, 64, 128)


def dot(a, b, dims):
    return lax.dot_general(a, b, dims, preferred_element_type=jnp.float32)


def aligned(x, m):
    return x if isinstance(x, int) else pl.multiple_of(x, m)


def wide(rows):
    return jnp.concatenate([rows[k : k + 1, :] for k in range(rows.shape[0])], axis=1)


def log_total(values):
    peak = functools.reduce(jnp.maximum, values)
    total = functools.reduce(jnp.add, [jnp.exp2(v - peak) for v in values])
    return peak + jnp.log(total) * LOG2E


def kernel(
    sq_hbm, tq_hbm, sp_hbm, tp_hbm, pos_ref, loss_ref, out, pas,
    sq, tq, sp, tp, es, et, stat, bs0, bt0, mx0, bs1, bt1, mx1, g, own, half, rfar, rnear, rx, ps, pr,
    sb1, s1, sb2, s2, lse, lb1, lb2, lb3, lacc, ssem, rsem, lsem,
):
    queries, ds = sq.shape
    passages, dt = tp.shape
    cs = LOGIT_GAIN / math.sqrt(ds) * LOG2E
    ct = LOGIT_GAIN / math.sqrt(dt) * LOG2E
    scale = LOGIT_GAIN / math.sqrt(ds)
    tiles = passages // TILE
    p, q = lax.axis_index("pass"), lax.axis_index("qry")
    core, y, z, xh = p % 2, (p // 2) % 4, (p // 8) % 4, p // 32

    def dev(c=core, yy=y, zz=z, x=xh, qq=q):
        return (((x * 4 + zz) * 4 + yy) * 2 + c, qq)

    loads = {}

    def load(name, src, dst):
        loads[name] = pltpu.make_async_copy(src, dst, lsem.at[len(loads)])
        loads[name].start()

    def rows(c):
        return pl.ds(c * CHUNK, CHUNK)

    load("sp", sp_hbm, sp)
    load("sq0", sq_hbm.at[rows(0)], sq.at[rows(0)])
    load("tp", tp_hbm, tp)
    load("tq0", tq_hbm.at[rows(0)], tq.at[rows(0)])
    for c in range(1, CHUNKS):
        load(f"sq{c}", sq_hbm.at[rows(c)], sq.at[rows(c)])
        load(f"tq{c}", tq_hbm.at[rows(c)], tq.at[rows(c)])

    group1 = [(a, b) for a in range(2) for b in range(4) if (a, b) != (0, 0)]
    peers1 = [dev(c=(core + a) % 2, yy=(y + b) % 4) for a, b in group1]
    peers2 = [dev(x=(xh + a) % 2, zz=(z + b) % 4) for a, b in group1]
    partner = dev(c=1 - core)
    across = dev(x=1 - xh)
    other = dev(qq=1 - q)
    barrier = pltpu.get_barrier_semaphore()
    everyone = peers1 + peers2 + [other]
    for peer in everyone:
        pl.semaphore_signal(barrier, inc=1, device_id=peer, device_id_type=MESH)

    counts = {"sem": 0}
    sent = []

    def sem():
        counts["sem"] += 1
        return counts["sem"] - 1

    def send(src, dst, peer, i=None):
        i = sem() if i is None else i
        copy = pltpu.make_async_remote_copy(
            src_ref=src, dst_ref=dst, send_sem=ssem.at[i], recv_sem=rsem.at[i], device_id=peer, device_id_type=MESH
        )
        copy.start()
        return copy

    def post(src, dst, peer):
        copy = send(src, dst, peer)
        sent.append(copy)
        return copy

    def spread(src, slots, peers, each):
        i = sem()
        for n, peer in enumerate(peers):
            send(src, each(n), peer, i)
        whole = slots.at[pl.ds(0, STATS - 1)]
        both = pltpu.make_async_remote_copy(
            src_ref=whole, dst_ref=whole, send_sem=ssem.at[i], recv_sem=rsem.at[i], device_id=peers[0], device_id_type=MESH
        )
        sent.append(both)
        return both

    buffers = ((bs0, bt0, mx0), (bs1, bt1, mx1))

    def products(i, piece):
        c, t = divmod(i, tiles)
        bs, bt, mx = buffers[i % 2]
        teacher, j = divmod(piece, 2)
        w = CHUNK // 2
        if t == 0 and j == 0:
            if c == 0:
                loads["tp" if teacher else "sp"].wait()
            loads[f"{'tq' if teacher else 'sq'}{c}"].wait()
        a = (tp if teacher else sp)[pl.ds(t * TILE, TILE), :]
        b = (tq if teacher else sq)[pl.ds(c * CHUNK + j * w, w), :]
        r = dot(a, b, NT)
        (bt if teacher else bs)[:, j * w : (j + 1) * w] = r
        mx[teacher, :, j * w : (j + 1) * w] = jnp.max(r.reshape(TILE // 8, 8, w), axis=0)

    def exponentials(i, j):
        c, t = divmod(i, tiles)
        bs, bt, mx = buffers[i % 2]
        w = CHUNK // 2
        cut = slice(j * w, (j + 1) * w)
        d = pl.ds(c * CHUNK + j * w, w)
        s2 = bs[:, cut] * cs
        t2 = bt[:, cut] * ct
        ms = jnp.max(mx[0, :, cut], axis=0, keepdims=True) * cs
        mt = jnp.max(mx[1, :, cut], axis=0, keepdims=True) * ct
        e_s = jnp.exp2(s2 - ms)
        e_t = jnp.exp2(t2 - mt)
        row = lax.broadcasted_iota(jnp.int32, (TILE, w), 0) + t * TILE
        at_positive = jnp.where(row == pos_ref[0:1, d] - p * passages, s2, 0.0)
        es[pl.ds(t * TILE, TILE), d] = e_s
        et[pl.ds(t * TILE, TILE), d] = e_t
        stat[t, 0:1, d] = ms
        stat[t, 1:2, d] = mt
        stat[t, 2:3, d] = jnp.sum(e_s, axis=0, keepdims=True)
        stat[t, 3:4, d] = jnp.sum(e_t, axis=0, keepdims=True)
        stat[t, 4:5, d] = jnp.sum(e_t * (t2 - s2), axis=0, keepdims=True)
        stat[t, 5:6, d] = jnp.sum(at_positive, axis=0, keepdims=True)

    def logits(c):
        for i in range(c * tiles, (c + 1) * tiles):
            for j in range(4):
                if i + 1 < CHUNKS * tiles:
                    products(i + 1, j)
                if j % 2 == 0:
                    exponentials(i, j // 2)

    waits1, waits2 = {}, {}
    per = CHUNKS // ROUNDS

    def stats_local(r):
        for n in range(per):
            d = rows(r * per + n)
            for k in range(2):
                peaks = [stat[t, k : k + 1, d] for t in range(tiles)]
                sums = [stat[t, 2 + k : 3 + k, d] for t in range(tiles)]
                peak = functools.reduce(jnp.maximum, peaks)
                total = functools.reduce(jnp.add, [s * jnp.exp2(m - peak) for s, m in zip(sums, peaks)])
                value = peak + jnp.log(total) * LOG2E
                for m in range(4):
                    at = (k * per + n) * 4 + m
                    sb1[r, at : at + 1, :] = value[:, m * 128 : (m + 1) * 128]
        waits1[r] = spread(sb1.at[r], s1.at[r], peers1, lambda n: s1.at[r, n])

    def stats_middle(r):
        waits1[r].wait_recv()
        sb2[r] = log_total([sb1[r]] + [s1[r, n] for n in range(STATS - 1)])
        waits2[r] = spread(sb2.at[r], s2.at[r], peers2, lambda n: s2.at[r, n])

    def stats_final(r):
        waits2[r].wait_recv()
        lse[r] = log_total([sb2[r]] + [s2[r, n] for n in range(STATS - 1)])
        for n in range(per):
            c = r * per + n
            d = rows(c)
            lse_s = wide(lse[r, n * 4 : n * 4 + 4, :])
            lse_t = wide(lse[r, (per + n) * 4 : (per + n) * 4 + 4, :])
            part = (1.5 * lse_s - lse_t) * (1.0 / 64.0)
            for t in range(tiles):
                part = part + stat[t, 4:5, d] * jnp.exp2(stat[t, 1:2, d] - lse_t) - CE_WEIGHT * stat[t, 5:6, d]
                stat[t, 6:7, d] = (1.0 + CE_WEIGHT) * jnp.exp2(stat[t, 0:1, d] - lse_s)
                stat[t, 7:8, d] = jnp.exp2(stat[t, 1:2, d] - lse_t)
            lacc[c : c + 1, :] = part

    def logit_grads(c):
        d = rows(c)
        positive = pos_ref[0:1, d] - p * passages

        @pl.loop(0, tiles)
        def _(t):
            r = pl.ds(pl.multiple_of(t * TILE, TILE), TILE)
            row = lax.broadcasted_iota(jnp.int32, (TILE, CHUNK), 0) + t * TILE
            v = es[r, d] * stat[t, 6:7, d] - et[r, d] * stat[t, 7:8, d]
            g[r, d] = jnp.where(row == positive, v - CE_WEIGHT, v).astype(jnp.bfloat16)

    def query_terms(c):
        own[rows(c), :] = dot(g[:, rows(c)], sp[...], TN)

    pas_rows = passages // 2
    pas_sent = []

    def passage_terms(into, first, b, r):
        n, k = TILE, queries // ROUNDS
        at = pl.ds(pl.multiple_of(first + b * n, n), n)
        term = dot(g[at, pl.ds(r * k, k)], sq[pl.ds(r * k, k), :], NN)
        to = pl.ds(b * n, n)
        into[to, :] = term if r == 0 else into[to, :] + term

    def passage_send(b, r):
        passage_terms(ps, (1 - q) * pas_rows, b, r)

    def passage_own(b, r):
        passage_terms(pas, q * pas_rows, b, r)

    def passage_post(n):
        r = pl.ds(sum(PARTS[:n]), PARTS[n])
        pas_sent.append(post(ps.at[r], pr.at[r], other))

    def passage_add(n):
        pas_sent[n].wait_recv()
        r = pl.ds(sum(PARTS[:n]), PARTS[n])
        pas[r, :] = (pas[r, :] + pr[r, :]) * (scale * passages * lax.axis_size("pass"))

    size = queries // CHUNKS
    piece, block, slab = size // 16, size // 64, size // 4
    hp = piece // 2

    def query_sum(c):
        base = c * size // 2

        def cut(s, j, h=None):
            at = base + s * slab + j * piece + (0 if h is None else h * hp)
            return half.at[pl.ds(aligned(at, hp), piece if h is None else hp)]

        def add(ref, *others):
            ref[...] = functools.reduce(jnp.add, [o[...] for o in others], ref[...])

        def far(s, k):
            return rfar.at[pl.ds(((c * 2 + s) * 6 + k) * hp, hp)]

        index = ((y, z), (z, y))

        def step(s, axis, d):
            along_y = (s == 0) == (axis == 0)
            return dev(yy=(y + d) % 4) if along_y else dev(zz=(z + d) % 4)

        first = post(
            own.at[pl.ds(aligned(c * size + (1 - core) * (size // 2), size // 2), size // 2)],
            half.at[pl.ds(base, size // 2)],
            partner,
        )
        yield
        first.wait_recv()
        mine = pl.ds(aligned(c * size + core * (size // 2), size // 2), size // 2)
        half[pl.ds(base, size // 2), :] = half[pl.ds(base, size // 2), :] + own[mine, :]
        w = {}
        for s in range(2):
            i = index[s][0]
            right, left = step(s, 0, 1), step(s, 0, 3)
            w[s, 0] = post(cut(s, (i + 2) % 4, 0), far(s, 0), right)
            w[s, 1] = post(cut(s, (i + 2) % 4, 1), far(s, 1), left)
            w[s, 2] = post(cut(s, (i + 1) % 4, 1), far(s, 2), right)
            w[s, 3] = post(cut(s, (i + 3) % 4, 0), far(s, 3), left)
        yield
        for s in range(2):
            i = index[s][0]
            right, left = step(s, 0, 1), step(s, 0, 3)
            w[s, 0].wait_recv()
            add(cut(s, (i + 1) % 4, 0), far(s, 0))
            w[s, 4] = post(cut(s, (i + 1) % 4, 0), far(s, 4), right)
            w[s, 1].wait_recv()
            add(cut(s, (i + 3) % 4, 1), far(s, 1))
            w[s, 5] = post(cut(s, (i + 3) % 4, 1), far(s, 5), left)
        yield

        def near(s, d):
            return rnear.at[pl.ds(((c * 2 + s) * 3 + d - 1) * block, block)]

        def small(s, j):
            at = base + s * slab + index[s][0] * piece + j * block
            return half.at[pl.ds(aligned(at, block), block)]

        for s in range(2):
            i, j = index[s]
            for k in range(2, 6):
                w[s, k].wait_recv()
            add(cut(s, i, 0), far(s, 3), far(s, 4))
            add(cut(s, i, 1), far(s, 2), far(s, 5))
            for d in range(1, 4):
                w[s, 5 + d] = post(small(s, (j + d) % 4), near(s, d), step(s, 1, d))
        yield

        def over(s):
            return rx.at[pl.ds((c * 2 + s) * block, block)]

        for s in range(2):
            j = index[s][1]
            for d in range(1, 4):
                w[s, 5 + d].wait_recv()
            add(small(s, j), *[near(s, d) for d in range(1, 4)])
            w[s, 9] = post(small(s, j), over(s), across)
        passage_post(len(pas_sent))
        yield

        def place(s, i, j=0, n=piece):
            at = c * size + core * (size // 2) + s * slab + i * piece + j * block
            return out.at[pl.ds(aligned(at, min(n, block)), n)]

        for s in range(2):
            i, j = index[s]
            w[s, 9].wait_recv()
            here = place(s, i, j, block)
            here[...] = (small(s, j)[...] + over(s)[...]) * scale
            for d in range(1, 4):
                w[s, 9 + d] = post(here, here, step(s, 1, d))
        yield
        for s in range(2):
            i = index[s][0]
            for d in range(1, 4):
                w[s, 9 + d].wait_recv()
            w[s, 13] = post(place(s, i), place(s, i), step(s, 0, 1))
            w[s, 14] = post(place(s, i), place(s, i), step(s, 0, 3))
        yield

        def part(s, i, h):
            at = c * size + core * (size // 2) + s * slab + i * piece + h * hp
            return out.at[pl.ds(aligned(at, hp), hp)]

        for s in range(2):
            i = index[s][0]
            w[s, 13].wait_recv()
            w[s, 15] = post(part(s, (i + 3) % 4, 0), part(s, (i + 3) % 4, 0), step(s, 0, 1))
            w[s, 14].wait_recv()
            w[s, 16] = post(part(s, (i + 1) % 4, 1), part(s, (i + 1) % 4, 1), step(s, 0, 3))
        yield
        for s in range(2):
            w[s, 15].wait_recv()
            w[s, 16].wait_recv()
            done = out.at[pl.ds(aligned(c * size + core * (size // 2) + s * slab, slab), slab)]
            w[s, 17] = post(done, done, partner)
        yield
        for s in range(2):
            w[s, 17].wait_recv()
        yield

    def loss_sum():
        i1, i2 = core * 4 + y, xh * 4 + z
        total = jnp.sum(lacc[0:CHUNKS, :], axis=0, keepdims=True)
        total = functools.reduce(jnp.add, [total[:, n * 128 : (n + 1) * 128] for n in range(CHUNK // 128)])
        lb1[i1] = jnp.broadcast_to(total, (8, 128))
        wait = spread(lb1.at[i1], lb1, peers1, lambda n: lb1.at[i1])
        yield
        wait.wait_recv()
        lb2[i2] = functools.reduce(jnp.add, [lb1[n] for n in range(STATS)])
        wait = spread(lb2.at[i2], lb2, peers2, lambda n: lb2.at[i2])
        yield
        wait.wait_recv()
        lb3[0] = functools.reduce(jnp.add, [lb2[n] for n in range(STATS)])
        last = post(lb3.at[0], lb3.at[1], other)
        yield
        last.wait_recv()
        value = jnp.sum(lb3[0, 0:1, :] + lb3[1, 0:1, :], axis=1, keepdims=True) * (LN2 / (2 * queries))
        loss_ref[...] = jnp.broadcast_to(value, loss_ref.shape)
        yield

    sums = [query_sum(c) for c in range(CHUNKS)]
    loss = loss_sum()
    for j in range(4):
        products(0, j)
    logits(0)
    logits(1)
    pl.semaphore_wait(barrier, len(everyone))
    stats_local(0)
    logits(2)
    stats_middle(0)
    logits(3)
    stats_local(1)
    stats_final(0)
    logit_grads(0)
    query_terms(0)
    next(sums[0])
    logit_grads(1)
    query_terms(1)
    next(sums[1])
    stats_middle(1)
    next(sums[0])
    passage_send(0, 0)
    passage_send(1, 0)
    next(sums[1])
    passage_own(0, 0)
    passage_own(1, 0)
    next(sums[0])
    stats_final(1)
    logit_grads(2)
    logit_grads(3)
    passage_send(0, 1)
    passage_post(0)
    passage_send(1, 1)
    next(sums[1])
    query_terms(2)
    next(sums[2])
    query_terms(3)
    next(sums[3])
    next(sums[0])
    passage_own(0, 1)
    next(sums[2])
    passage_own(1, 1)
    next(sums[1])
    next(sums[3])
    stages = {0: 4, 1: 4, 2: 2, 3: 2}
    for tick in range(4, 20):
        for c in range(CHUNKS):
            while stages[c] < 10 and stages[c] + c <= tick:
                next(sums[c])
                stages[c] += 1
        if 7 <= tick < 11:
            next(loss)
    for n in range(len(PARTS)):
        passage_add(n)
    for copy in sent:
        copy.wait_send()


def shards(student_queries, teacher_queries, student_passages, teacher_passages, positives):
    queries, ds = student_queries.shape
    passages, dt = teacher_passages.shape
    f32, bf16 = jnp.float32, jnp.bfloat16
    vmem = pltpu.VMEM
    size = queries // CHUNKS
    scratch = [
        vmem((queries, ds), bf16),
        vmem((queries, dt), bf16),
        vmem((passages, ds), bf16),
        vmem((passages, dt), bf16),
        vmem((passages, queries), f32),
        vmem((passages, queries), f32),
        vmem((passages // TILE, 8, queries), f32),
        *[vmem((TILE, CHUNK), f32), vmem((TILE, CHUNK), f32), vmem((2, 8, CHUNK), f32)] * 2,
        vmem((passages, queries), bf16),
        vmem((queries, ds), f32),
        vmem((queries // 2, ds), f32),
        vmem((CHUNKS * 2 * 6 * (size // 32), ds), f32),
        vmem((CHUNKS * 2 * 3 * (size // 64), ds), f32),
        vmem((CHUNKS * 2 * (size // 64), ds), f32),
        vmem((passages // 2, ds), f32),
        vmem((passages // 2, ds), f32),
        vmem((ROUNDS, 16, 128), f32),
        vmem((ROUNDS, STATS - 1, 16, 128), f32),
        vmem((ROUNDS, 16, 128), f32),
        vmem((ROUNDS, STATS - 1, 16, 128), f32),
        vmem((ROUNDS, 16, 128), f32),
        vmem((STATS, 8, 128), f32),
        vmem((STATS, 8, 128), f32),
        vmem((2, 8, 128), f32),
        vmem((8, CHUNK), f32),
        pltpu.SemaphoreType.DMA((180,)),
        pltpu.SemaphoreType.DMA((180,)),
        pltpu.SemaphoreType.DMA((2 + 2 * CHUNKS,)),
    ]
    loss, query_grads, passage_grads = pl.pallas_call(
        kernel,
        out_shape=(
            jax.ShapeDtypeStruct((8, 128), f32),
            vmem((queries, ds), f32),
            vmem((passages // 2, ds), f32),
        ),
        in_specs=[pl.BlockSpec(memory_space=pl.ANY)] * 4 + [pl.BlockSpec(memory_space=vmem)],
        out_specs=[pl.BlockSpec(memory_space=vmem)] * 3,
        scratch_shapes=scratch,
        compiler_params=pltpu.CompilerParams(collective_id=0, has_side_effects=True, vmem_limit_bytes=52 * 2**20),
        cost_estimate=pl.CostEstimate(flops=14 * 10**9, bytes_accessed=20 * 10**6, transcendentals=4 * 10**6),
    )(student_queries, teacher_queries, student_passages, teacher_passages, positives.reshape(1, queries))
    return loss[0, 0], query_grads, passage_grads


def solution(mesh):
    return jax.shard_map(
        shards,
        mesh=mesh,
        in_specs=(P("qry", None), P("qry", None), P("pass", None), P("pass", None), P("qry")),
        out_specs=(P(), P("qry", None), P(("pass", "qry"), None)),
        check_vma=False,
    )
```

```python
import functools
import math

import jax
import jax.numpy as jnp
from jax import lax
from jax.experimental import pallas as pl
from jax.experimental.pallas import tpu as pltpu
from jax.sharding import PartitionSpec as P

LOGIT_GAIN = 3.0
CE_WEIGHT = 0.5
LOG2E = math.log2(math.e)
LN2 = math.log(2.0)
MESH = pl.DeviceIdType.MESH
NT = (((1,), (1,)), ((), ()))
TN = (((0,), (0,)), ((), ()))
NN = (((1,), (0,)), ((), ()))
TILE = 256
CHUNK = 512
UNIT = 256
CHUNKS = 4
STATS = 8
ROUNDS = 2
EVENTS = (
    6, 0, 1, 7, 0, 2, 1, 3, 4, -64, 0, 2, 8, 1, -32, 3, 8, 9, 2, -32, 9, 9, 1, 3, -32, 9, 9, 0, 2, 9, 9, 9, 3, 0, -32,
    5, 1, -32, 0, -32, 5, 2, -32, 3, 1, 0, -32, 5, 2, -32, 0, 3, 1, -32, 2, -32, 5, 3, -32, 1, 2, -32, 1, 3, 2, -32, 3,
)
PARTS = tuple(-e for e in EVENTS if e < 0)


def dot(a, b, dims):
    return lax.dot_general(a, b, dims, preferred_element_type=jnp.float32)


def aligned(x, m):
    return x if isinstance(x, int) else pl.multiple_of(x, m)


def wide(rows):
    return jnp.concatenate([rows[k : k + 1, :] for k in range(rows.shape[0])], axis=1)


def log_total(values):
    peak = functools.reduce(jnp.maximum, values)
    total = functools.reduce(jnp.add, [jnp.exp2(v - peak) for v in values])
    return peak + jnp.log(total) * LOG2E


def kernel(
    sq_hbm, tq_hbm, sp_hbm, tp_hbm, pos_ref, loss_ref, out, pas,
    sq, tq, sp, tp, raw_s, raw_t, peaks, totals, g, own, half, rfar, rnear, rx, ps, pr,
    sb1, s1, sb2, s2, lse, lses, lb1, lb2, lb3, lacc, ssem, rsem, lsem,
):
    queries, ds = sq.shape
    passages, dt = tp.shape
    cs = LOGIT_GAIN / math.sqrt(ds) * LOG2E
    ct = LOGIT_GAIN / math.sqrt(dt) * LOG2E
    scale = LOGIT_GAIN / math.sqrt(ds)
    tiles = passages // TILE
    units = 2 * (queries // UNIT)
    p, q = lax.axis_index("pass"), lax.axis_index("qry")
    core, y, z, xh = p % 2, (p // 2) % 4, (p // 8) % 4, p // 32

    def dev(c=core, yy=y, zz=z, x=xh, qq=q):
        return (((x * 4 + zz) * 4 + yy) * 2 + c, qq)

    loads = {}

    def load(name, src, dst):
        loads[name] = pltpu.make_async_copy(src, dst, lsem.at[len(loads)])
        loads[name].start()

    def rows(c):
        return pl.ds(c * CHUNK, CHUNK)

    def unit(b):
        return pl.ds(b * UNIT, UNIT)

    top, bottom = pl.ds(0, passages // 2), pl.ds(passages // 2, passages // 2)
    load("s0", sp_hbm.at[top], sp.at[top])
    load("sq0", sq_hbm.at[unit(0)], sq.at[unit(0)])
    load("s1", sp_hbm.at[bottom], sp.at[bottom])
    load("t0", tp_hbm.at[top], tp.at[top])
    load("tq0", tq_hbm.at[unit(0)], tq.at[unit(0)])
    load("t1", tp_hbm.at[bottom], tp.at[bottom])
    load("sq1", sq_hbm.at[unit(1)], sq.at[unit(1)])
    load("tq1", tq_hbm.at[unit(1)], tq.at[unit(1)])
    for c in range(1, CHUNKS):
        load(f"sq{2 * c}", sq_hbm.at[rows(c)], sq.at[rows(c)])
        load(f"tq{2 * c}", tq_hbm.at[rows(c)], tq.at[rows(c)])

    group1 = [(a, b) for a in range(2) for b in range(4) if (a, b) != (0, 0)]
    peers1 = [dev(c=(core + a) % 2, yy=(y + b) % 4) for a, b in group1]
    peers2 = [dev(x=(xh + a) % 2, zz=(z + b) % 4) for a, b in group1]
    partner = dev(c=1 - core)
    across = dev(x=1 - xh)
    other = dev(qq=1 - q)
    barrier = pltpu.get_barrier_semaphore()
    everyone = peers1 + peers2 + [other]
    for peer in everyone:
        pl.semaphore_signal(barrier, inc=1, device_id=peer, device_id_type=MESH)

    counts = {"sem": 0}
    sent = []

    def sem():
        counts["sem"] += 1
        return counts["sem"] - 1

    def send(src, dst, peer, i=None):
        i = sem() if i is None else i
        copy = pltpu.make_async_remote_copy(
            src_ref=src, dst_ref=dst, send_sem=ssem.at[i], recv_sem=rsem.at[i], device_id=peer, device_id_type=MESH
        )
        copy.start()
        return copy

    def post(src, dst, peer):
        copy = send(src, dst, peer)
        sent.append(copy)
        return copy

    def spread(src, slots, peers, each):
        i = sem()
        for n, peer in enumerate(peers):
            send(src, each(n), peer, i)
        whole = slots.at[pl.ds(0, STATS - 1)]
        both = pltpu.make_async_remote_copy(
            src_ref=whole, dst_ref=whole, send_sem=ssem.at[i], recv_sem=rsem.at[i], device_id=peers[0], device_id_type=MESH
        )
        sent.append(both)
        return both

    raws, sides, factors = (raw_s, raw_t), ((sp, sq), (tp, tq)), (cs, ct)

    def products(u, j):
        b, k = divmod(u, 2)
        if b == 0:
            loads[f"{'st'[k]}{j}"].wait()
        if j == 0 and f"{'st'[k]}q{b}" in loads:
            loads[f"{'st'[k]}q{b}"].wait()
        half_rows = pl.ds(j * (passages // 2), passages // 2)
        d = unit(b)
        r = dot(sides[k][0][half_rows, :], sides[k][1][d, :], NT)
        raws[k][half_rows, d] = r
        m = jnp.max(r.reshape(passages // 16, 8, UNIT), axis=0)
        peaks[k, :, d] = m if j == 0 else jnp.maximum(peaks[k, :, d], m)

    def exponentials(u, j):
        b, k = divmod(u, 2)
        d = unit(b)
        m = jnp.max(peaks[k, :, d], axis=0, keepdims=True) * factors[k]
        e = jnp.exp2(raws[k][pl.ds(j * TILE, TILE), d] * factors[k] - m)
        total = jnp.sum(e.reshape(TILE // 8, 8, UNIT), axis=0)
        totals[k, :, d] = total if j == 0 else totals[k, :, d] + total

    def logits(u):
        for j in range(tiles):
            if u < units and j % 2 == 0:
                products(u, j // 2)
            if u > 0:
                exponentials(u - 1, j)

    waits1, waits2 = {}, {}

    def stats_local(r):
        n = queries // ROUNDS
        d = pl.ds(r * n, n)
        for k in range(2):
            peak = jnp.max(peaks[k, :, d], axis=0, keepdims=True) * factors[k]
            value = peak + jnp.log(jnp.sum(totals[k, :, d], axis=0, keepdims=True)) * LOG2E
            for m in range(n // 128):
                at = k * (n // 128) + m
                sb1[r, at : at + 1, :] = value[:, m * 128 : (m + 1) * 128]
        waits1[r] = spread(sb1.at[r], s1.at[r], peers1, lambda n: s1.at[r, n])

    def stats_middle(r):
        waits1[r].wait_recv()
        sb2[r] = log_total([sb1[r]] + [s1[r, n] for n in range(STATS - 1)])
        waits2[r] = spread(sb2.at[r], s2.at[r], peers2, lambda n: s2.at[r, n])

    def stats_final(r):
        waits2[r].wait_recv()
        lse[r] = log_total([sb2[r]] + [s2[r, n] for n in range(STATS - 1)])
        n = queries // ROUNDS
        for k in range(2):
            lses[k : k + 1, pl.ds(r * n, n)] = wide(lse[r, k * (n // 128) : (k + 1) * (n // 128), :])

    def logit_grads(c, t):
        d = rows(c)
        start = t * TILE if isinstance(t, int) else pl.multiple_of(t * TILE, TILE)
        r = pl.ds(start, TILE)
        row = lax.broadcasted_iota(jnp.int32, (TILE, CHUNK), 0)
        positive = pos_ref[0:1, d] - (p * passages + start)
        student = jnp.exp2(raw_s[r, d] * cs - (lses[0:1, d] - math.log2(1.0 + CE_WEIGHT)))
        teacher = jnp.exp2(raw_t[r, d] * ct - lses[1:2, d])
        v = student - teacher
        g[r, d] = jnp.where(row == positive, v - CE_WEIGHT, v).astype(jnp.bfloat16)

    def query_terms(c, n):
        w = ds // 3
        own[rows(c), n * w : (n + 1) * w] = dot(g[:, rows(c)], sp[:, n * w : (n + 1) * w], TN)

    def loss_terms(i):
        c, t = divmod(i, tiles)
        d, r = rows(c), pl.ds(t * TILE, TILE)
        row = lax.broadcasted_iota(jnp.int32, (TILE, CHUNK), 0)
        positive = pos_ref[0:1, d] - (p * passages + t * TILE)
        s2, t2 = raw_s[r, d] * cs, raw_t[r, d] * ct
        v = jnp.exp2(t2 - lses[1:2, d]) * (t2 - s2)
        v = jnp.where(row == positive, v - CE_WEIGHT * s2, v)
        v = jnp.sum(v.reshape(TILE // 8, 8, CHUNK), axis=0)
        lacc[...] = v if i == 0 else lacc[...] + v

    pas_rows = passages // 2
    pas_sent = []

    def passage_terms(into, first, b, r):
        n, k = TILE, queries // ROUNDS
        at = pl.ds(pl.multiple_of(first + b * n, n), n)
        to = pl.ds(b * n, n)
        if r is None:
            into[to, :] = dot(g[at, :], sq[...], NN)
        else:
            term = dot(g[at, pl.ds(r * k, k)], sq[pl.ds(r * k, k), :], NN)
            into[to, :] = term if r == 0 else into[to, :] + term

    def passage_send(b, r):
        passage_terms(ps, (1 - q) * pas_rows, b, r)

    def passage_own(b):
        passage_terms(pas, q * pas_rows, b, None)

    def passage_post(n):
        r = pl.ds(sum(PARTS[:n]), PARTS[n])
        pas_sent.append(post(ps.at[r], pr.at[r], other))

    def passage_add(n):
        pas_sent[n].wait_recv()
        r = pl.ds(sum(PARTS[:n]), PARTS[n])
        pas[r, :] = (pas[r, :] + pr[r, :]) * (scale * passages * lax.axis_size("pass"))

    size = queries // CHUNKS
    piece, block, slab = size // 16, size // 64, size // 4
    hp = piece // 2

    def query_sum(c):
        base = c * size // 2

        def cut(s, j, h=None):
            at = base + s * slab + j * piece + (0 if h is None else h * hp)
            return half.at[pl.ds(aligned(at, hp), piece if h is None else hp)]

        def add(ref, *others):
            ref[...] = functools.reduce(jnp.add, [o[...] for o in others], ref[...])

        def far(s, k):
            return rfar.at[pl.ds(((c * 2 + s) * 6 + k) * hp, hp)]

        index = ((y, z), (z, y))

        def step(s, axis, d):
            along_y = (s == 0) == (axis == 0)
            return dev(yy=(y + d) % 4) if along_y else dev(zz=(z + d) % 4)

        first = post(
            own.at[pl.ds(aligned(c * size + (1 - core) * (size // 2), size // 2), size // 2)],
            half.at[pl.ds(base, size // 2)],
            partner,
        )
        yield
        first.wait_recv()
        mine = pl.ds(aligned(c * size + core * (size // 2), size // 2), size // 2)
        half[pl.ds(base, size // 2), :] = half[pl.ds(base, size // 2), :] + own[mine, :]
        w = {}
        for s in range(2):
            i = index[s][0]
            right, left = step(s, 0, 1), step(s, 0, 3)
            w[s, 0] = post(cut(s, (i + 2) % 4, 0), far(s, 0), right)
            w[s, 1] = post(cut(s, (i + 2) % 4, 1), far(s, 1), left)
            w[s, 2] = post(cut(s, (i + 1) % 4, 1), far(s, 2), right)
            w[s, 3] = post(cut(s, (i + 3) % 4, 0), far(s, 3), left)
        yield
        for s in range(2):
            i = index[s][0]
            right, left = step(s, 0, 1), step(s, 0, 3)
            w[s, 0].wait_recv()
            add(cut(s, (i + 1) % 4, 0), far(s, 0))
            w[s, 4] = post(cut(s, (i + 1) % 4, 0), far(s, 4), right)
            w[s, 1].wait_recv()
            add(cut(s, (i + 3) % 4, 1), far(s, 1))
            w[s, 5] = post(cut(s, (i + 3) % 4, 1), far(s, 5), left)
        yield

        def near(s, d):
            return rnear.at[pl.ds(((c * 2 + s) * 3 + d - 1) * block, block)]

        def small(s, j):
            at = base + s * slab + index[s][0] * piece + j * block
            return half.at[pl.ds(aligned(at, block), block)]

        for s in range(2):
            i, j = index[s]
            for k in range(2, 6):
                w[s, k].wait_recv()
            add(cut(s, i, 0), far(s, 3), far(s, 4))
            add(cut(s, i, 1), far(s, 2), far(s, 5))
            for d in range(1, 4):
                w[s, 5 + d] = post(small(s, (j + d) % 4), near(s, d), step(s, 1, d))
        yield

        def over(s):
            return rx.at[pl.ds((c * 2 + s) * block, block)]

        for s in range(2):
            j = index[s][1]
            for d in range(1, 4):
                w[s, 5 + d].wait_recv()
            add(small(s, j), *[near(s, d) for d in range(1, 4)])
            w[s, 9] = post(small(s, j), over(s), across)
        yield

        def place(s, i, j=0, n=piece):
            at = c * size + core * (size // 2) + s * slab + i * piece + j * block
            return out.at[pl.ds(aligned(at, min(n, block)), n)]

        for s in range(2):
            i, j = index[s]
            w[s, 9].wait_recv()
            here = place(s, i, j, block)
            here[...] = (small(s, j)[...] + over(s)[...]) * scale
            for d in range(1, 4):
                w[s, 9 + d] = post(here, here, step(s, 1, d))
        yield
        for s in range(2):
            i = index[s][0]
            for d in range(1, 4):
                w[s, 9 + d].wait_recv()
            w[s, 13] = post(place(s, i), place(s, i), step(s, 0, 1))
            w[s, 14] = post(place(s, i), place(s, i), step(s, 0, 3))
        yield

        def part(s, i, h):
            at = c * size + core * (size // 2) + s * slab + i * piece + h * hp
            return out.at[pl.ds(aligned(at, hp), hp)]

        for s in range(2):
            i = index[s][0]
            w[s, 13].wait_recv()
            w[s, 15] = post(part(s, (i + 3) % 4, 0), part(s, (i + 3) % 4, 0), step(s, 0, 1))
            w[s, 14].wait_recv()
            w[s, 16] = post(part(s, (i + 1) % 4, 1), part(s, (i + 1) % 4, 1), step(s, 0, 3))
        yield
        for s in range(2):
            w[s, 15].wait_recv()
            w[s, 16].wait_recv()
            done = out.at[pl.ds(aligned(c * size + core * (size // 2) + s * slab, slab), slab)]
            w[s, 17] = post(done, done, partner)
        yield
        for s in range(2):
            w[s, 17].wait_recv()
        yield

    def loss_sum():
        i1, i2 = core * 4 + y, xh * 4 + z
        own_share = (1.5 * lses[0:1, :] - lses[1:2, :]) * (1.0 / 64.0)
        total = jnp.sum(lacc[...], axis=0, keepdims=True)
        total = functools.reduce(
            jnp.add,
            [total[:, n * 128 : (n + 1) * 128] for n in range(CHUNK // 128)]
            + [own_share[:, n * 128 : (n + 1) * 128] for n in range(queries // 128)],
        )
        lb1[i1] = jnp.broadcast_to(total, (8, 128))
        wait = spread(lb1.at[i1], lb1, peers1, lambda n: lb1.at[i1])
        yield
        wait.wait_recv()
        lb2[i2] = functools.reduce(jnp.add, [lb1[n] for n in range(STATS)])
        wait = spread(lb2.at[i2], lb2, peers2, lambda n: lb2.at[i2])
        yield
        wait.wait_recv()
        lb3[0] = functools.reduce(jnp.add, [lb2[n] for n in range(STATS)])
        last = post(lb3.at[0], lb3.at[1], other)
        yield
        last.wait_recv()
        value = jnp.sum(lb3[0, 0:1, :] + lb3[1, 0:1, :], axis=1, keepdims=True) * (LN2 / (2 * queries))
        loss_ref[...] = value
        yield

    sums = [query_sum(c) for c in range(CHUNKS)]
    loss = loss_sum()
    logits(0)
    for u in range(1, units + 1):
        logits(u)
        if u == units // 2:
            pl.semaphore_wait(barrier, len(everyone))
            stats_local(0)
        if u == units - 2:
            stats_middle(0)
    stats_local(1)
    stats_final(0)
    for t in range(tiles):
        logit_grads(0, t)
    for t in range(tiles):
        if t < 3:
            query_terms(0, t)
        logit_grads(1, t)
    next(sums[0])
    stats_middle(1)
    for n in range(3):
        query_terms(1, n)
    next(sums[1])
    passage_send(0, 0)
    next(sums[0])
    passage_send(1, 0)
    stats_final(1)
    tiles_done, blocks_done = 0, 0
    for e in EVENTS:
        if e < 0:
            passage_post(len(pas_sent))
        elif e < 4:
            next(sums[e])
        elif e == 5:
            next(loss)
        elif e == 4:
            for t in range(2):
                passage_send(t, 1)
        elif e < 8:
            c = e - 4
            for t in range(tiles):
                logit_grads(c, t)
            for n in range(3):
                query_terms(c, n)
            next(sums[c])
        elif e == 8:
            passage_own(blocks_done)
            blocks_done += 1
        else:
            for _ in range(2):
                loss_terms(tiles_done)
                tiles_done += 1
    for n in range(len(PARTS)):
        passage_add(n)
    for copy in sent:
        copy.wait_send()


def shards(student_queries, teacher_queries, student_passages, teacher_passages, positives):
    queries, ds = student_queries.shape
    passages, dt = teacher_passages.shape
    f32, bf16 = jnp.float32, jnp.bfloat16
    vmem = pltpu.VMEM
    size = queries // CHUNKS
    scratch = [
        vmem((queries, ds), bf16),
        vmem((queries, dt), bf16),
        vmem((passages, ds), bf16),
        vmem((passages, dt), bf16),
        vmem((passages, queries), f32),
        vmem((passages, queries), f32),
        vmem((2, 8, queries), f32),
        vmem((2, 8, queries), f32),
        vmem((passages, queries), bf16),
        vmem((queries, ds), f32),
        vmem((queries // 2, ds), f32),
        vmem((CHUNKS * 2 * 6 * (size // 32), ds), f32),
        vmem((CHUNKS * 2 * 3 * (size // 64), ds), f32),
        vmem((CHUNKS * 2 * (size // 64), ds), f32),
        vmem((passages // 2, ds), f32),
        vmem((passages // 2, ds), f32),
        vmem((ROUNDS, 16, 128), f32),
        vmem((ROUNDS, STATS - 1, 16, 128), f32),
        vmem((ROUNDS, 16, 128), f32),
        vmem((ROUNDS, STATS - 1, 16, 128), f32),
        vmem((ROUNDS, 16, 128), f32),
        vmem((8, queries), f32),
        vmem((STATS, 8, 128), f32),
        vmem((STATS, 8, 128), f32),
        vmem((2, 8, 128), f32),
        vmem((8, CHUNK), f32),
        pltpu.SemaphoreType.DMA((180,)),
        pltpu.SemaphoreType.DMA((180,)),
        pltpu.SemaphoreType.DMA((16,)),
    ]
    loss, query_grads, passage_grads = pl.pallas_call(
        kernel,
        out_shape=(
            jax.ShapeDtypeStruct((1, 1), f32),
            vmem((queries, ds), f32),
            vmem((passages // 2, ds), f32),
        ),
        in_specs=[pl.BlockSpec(memory_space=pl.ANY)] * 4 + [pl.BlockSpec(memory_space=vmem)],
        out_specs=[pl.BlockSpec(memory_space=vmem)] * 3,
        scratch_shapes=scratch,
        compiler_params=pltpu.CompilerParams(collective_id=0, has_side_effects=True, vmem_limit_bytes=52 * 2**20),
        cost_estimate=pl.CostEstimate(flops=14 * 10**9, bytes_accessed=20 * 10**6, transcendentals=4 * 10**6),
    )(student_queries, teacher_queries, student_passages, teacher_passages, positives.reshape(1, queries))
    return loss.reshape(()), query_grads, passage_grads


def solution(mesh):
    return jax.shard_map(
        shards,
        mesh=mesh,
        in_specs=(P("qry", None), P("qry", None), P("pass", None), P("pass", None), P("qry")),
        out_specs=(P(), P("qry", None), P(("pass", "qry"), None)),
        check_vma=False,
    )
```
